32 devices in a mesh: seq: 8 (over z, x), batch: 4 (over y, core).
Axes of the slice: x: 2, y: 2, z: 4, core: 2. Of those that a mesh axis runs over, the one named last changes fastest.
Arguments:
- token_ids: int32 [4, 2048], P('batch', 'seq'), may hold values from 0 to 15
- input_table: bfloat16 [16, 3840], replicated, may hold values from -6 to 6
- gate_table: bfloat16 [16, 3584], replicated, may hold values from -6 to 6
- step_table: float32 [16, 56], replicated, may hold values from -4.5 to -1.5
- decay_log: float32 [56], replicated, may hold values from -12 to 0
- conv_weight: float32 [4, 3840], replicated, may hold values from -3 to 3
- conv_bias: float32 [3840], replicated, may hold values from -3 to 3
- skip_gain: float32 [56], replicated, may hold values from 0.25 to 1.75
- norm_gain: float32 [3584], replicated, may hold values from 0.5 to 1.5
- cotangent: bfloat16 [4, 2048, 3584], P('batch', 'seq'), may hold values from -1 to 1
Outputs:
- layer_out: bfloat16 [4, 2048, 3584], P('batch', 'seq')
- input_grad: float32 [16, 3840], replicated
- gate_grad: float32 [16, 3584], replicated
- step_grad: float32 [16, 56], replicated
- decay_grad: float32 [56], replicated
- conv_weight_grad: float32 [4, 3840], replicated
- conv_bias_grad: float32 [3840], replicated
- skip_grad: float32 [56], replicated
- norm_grad: float32 [3584], replicated
The draws below stay inside these ranges and needn't reach their ends.
All inputs are finite; a program needn't handle non-finite values.
Results may differ from the reference program's by a relative error of at most 0.014.
Values sent between devices are 32-bit elements; how exact they have to be, the bound alone decides.
A program may use at most 320 MiB of HBM per device.

```python
import math
from functools import partial
import jax
import jax.numpy as jnp
from jax import lax

VOCAB = 16
HEADS = 56
HEAD = 64
STATE = 128
CONV_WIDTH = 4
BLOCK = 128
TOK_DEV = 256
INNER = 3584
CONV = 3840
LENGTH = 2048
BATCH = 4


def draw_token_ids(key, part):
    blocks = LENGTH // TOK_DEV
    keys = jax.random.split(jax.random.fold_in(key, 3), 4)
    favoured = jax.random.randint(keys[0], (BATCH, blocks, 2), 0, VOCAB)
    which = jax.random.randint(keys[1], (BATCH, blocks, TOK_DEV), 0, 2)
    picks = jnp.take_along_axis(favoured, which, axis=2)
    spread = jax.random.randint(keys[2], (BATCH, blocks, TOK_DEV), 0, VOCAB)
    coin = jax.random.randint(keys[3], (BATCH, blocks, TOK_DEV), 0, 4)
    return jnp.where(coin == 0, spread, picks).reshape(BATCH, LENGTH).astype(jnp.int32)


def draw_decay_log(key, part):
    keys = jax.random.split(jax.random.fold_in(key, 11), 4)
    share = 0.5
    chosen = jax.random.randint(keys[3], (), 0, HEADS)
    slow = (jax.random.uniform(keys[0], (HEADS,), jnp.float32) < share) | (jnp.arange(HEADS) == chosen)
    slow_rate = jnp.exp(jax.random.uniform(keys[1], (HEADS,), jnp.float32, math.log(0.2), math.log(0.6))) / (0.07 * LENGTH)
    fast_rate = jnp.exp(jax.random.uniform(keys[2], (HEADS,), jnp.float32, math.log(1.0 / 50.0), math.log(1.0 / 30.0))) / 0.07
    return jnp.log(jnp.where(slow, slow_rate, fast_rate)).astype(jnp.float32)


def draw_cotangent(key, part):
    keys = jax.random.split(jax.random.fold_in(key, 5), 1)
    noise = jnp.clip(jax.random.normal(keys[0], (BATCH, LENGTH, INNER), jnp.float32), -4.0, 4.0)
    ramp = 1.0 + 2.0 * jnp.arange(LENGTH, dtype=jnp.float32) / LENGTH
    scale = 1.0 / math.sqrt(BATCH * LENGTH)
    result = noise * ramp[None, :, None]
    return (result * scale).astype(jnp.bfloat16)


def gaussian(key, shape, deviation, limit, kind=jnp.bfloat16):
    values = deviation * jax.random.normal(key, shape, jnp.float32)
    return jnp.clip(values, min=-limit, max=limit).astype(kind)


def setup_inputs(seed: int = 0) -> dict:
    arg_keys = jax.random.split(jax.random.key(seed), 11)
    return {
        "token_ids": draw_token_ids(jax.random.fold_in(arg_keys[10], 71), 0),
        "input_table": gaussian(arg_keys[1], (VOCAB, CONV), 1.0, 6.0),
        "gate_table": gaussian(arg_keys[2], (VOCAB, INNER), 1.0, 6.0),
        "step_table": jnp.clip(jax.random.uniform(arg_keys[3], (VOCAB, HEADS), jnp.float32, -4.5, -1.5), -4.5, -1.5),
        "decay_log": draw_decay_log(jax.random.fold_in(arg_keys[10], 71), 0),
        "conv_weight": gaussian(arg_keys[5], (CONV_WIDTH, CONV), CONV_WIDTH ** -0.5, 3.0, jnp.float32),
        "conv_bias": gaussian(arg_keys[6], (CONV,), 0.5, 3.0, jnp.float32),
        "skip_gain": jnp.clip(1.0 + 0.15 * jax.random.normal(arg_keys[7], (HEADS,), jnp.float32), 0.25, 1.75),
        "norm_gain": jnp.clip(1.0 + 0.1 * jax.random.normal(arg_keys[8], (INNER,), jnp.float32), 0.5, 1.5),
        "cotangent": draw_cotangent(jax.random.fold_in(arg_keys[10], 71), 0),
    }


EPS = 1e-05
HIGH = lax.Precision.HIGHEST

def indicator(labels, vocab):
    return (labels[:, None] == jnp.arange(vocab, dtype=jnp.int32)[None, :]).astype(jnp.float32)

def rounded(value):
    return lax.optimization_barrier(value.astype(jnp.bfloat16))

def group_step(carried, item):
    values, write_keys, read_keys, steps, log_decay = item
    cum = jnp.cumsum(log_decay, axis=0)
    last = cum[-1]
    reads = read_keys.astype(jnp.float32)
    writes = write_keys.astype(jnp.float32)
    vals = values.astype(jnp.float32)
    scores = jnp.einsum('tn,sn->ts', reads, writes)
    lower = (lax.broadcasted_iota(jnp.int32, (BLOCK, BLOCK), 0) >= lax.broadcasted_iota(jnp.int32, (BLOCK, BLOCK), 1))[None]
    track = cum.T
    power = track[:, :, None] - track[:, None, :]
    fade = jnp.where(lower, jnp.exp(jnp.where(lower, power, 0.0)), 0.0)
    mixing = rounded(scores[None] * fade * steps.T[:, None, :]).astype(jnp.float32)
    within = jnp.einsum('hts,shp->thp', mixing, vals)
    held = rounded(carried).astype(jnp.float32)
    across = jnp.exp(cum)[:, :, None] * jnp.einsum('tn,hpn->thp', reads, held)
    weighted = rounded(vals * (jnp.exp(last[None, :] - cum) * steps)[:, :, None]).astype(jnp.float32)
    fresh = jnp.einsum('shp,sn->hpn', weighted, writes)
    following = jnp.exp(last)[:, None, None] * carried + fresh
    return (following, within + across)

def sequence_forward(labels, params):
    input_t, gate_t, step_t, decay_log, conv_weight, conv_bias, skip_gain, norm_gain = params
    width = conv_weight.shape[0]
    padded = jnp.concatenate([jnp.full((width - 1,), -1, jnp.int32), labels.astype(jnp.int32)])
    raw = jnp.dot(indicator(padded, VOCAB), input_t, precision=HIGH)
    own = indicator(labels.astype(jnp.int32), VOCAB)
    gate_rows = jnp.dot(own, gate_t, precision=HIGH)
    step_rows = jnp.dot(own, step_t, precision=HIGH)
    convolved = conv_bias[None, :] + conv_weight[0][None, :] * raw[0:LENGTH]
    for offset in range(1, width):
        convolved = convolved + conv_weight[offset][None, :] * raw[offset:offset + LENGTH]
    active = jax.nn.silu(convolved)
    values = rounded(active[:, :INNER]).reshape(LENGTH, HEADS, HEAD)
    write_keys = rounded(active[:, INNER:INNER + STATE])
    read_keys = rounded(active[:, INNER + STATE:])
    steps = jax.nn.softplus(step_rows)
    log_decay = -jnp.exp(decay_log)[None, :] * steps
    count = LENGTH // BLOCK
    items = (values.reshape(count, BLOCK, HEADS, HEAD), write_keys.reshape(count, BLOCK, STATE), read_keys.reshape(count, BLOCK, STATE), steps.reshape(count, BLOCK, HEADS), log_decay.reshape(count, BLOCK, HEADS))
    start = jnp.zeros((HEADS, HEAD, STATE), jnp.float32)
    _, mixed = lax.scan(jax.checkpoint(group_step), start, items)
    mixed = mixed.reshape(LENGTH, HEADS, HEAD) + skip_gain[None, :, None] * values.astype(jnp.float32)
    gated = mixed.reshape(LENGTH, INNER) * jax.nn.silu(gate_rows)
    scale = lax.rsqrt(lax.optimization_barrier(jnp.mean(gated * gated, axis=1, keepdims=True)) + EPS)
    return (gated * scale * norm_gain[None, :]).astype(jnp.bfloat16)

def reference(token_ids, input_table, gate_table, step_table, decay_log, conv_weight, conv_bias, skip_gain, norm_gain, cotangent):
    params = (input_table.astype(jnp.float32), gate_table.astype(jnp.float32), step_table, decay_log, conv_weight, conv_bias, skip_gain, norm_gain)

    def per_sequence(totals, item):
        labels, sequence_cot = item
        produced, pull = jax.vjp(partial(sequence_forward, labels), params)
        grads = pull(sequence_cot)[0]
        return (jax.tree.map(jnp.add, totals, grads), produced)
    zeros = jax.tree.map(jnp.zeros_like, params)
    grads, produced = lax.scan(per_sequence, zeros, (token_ids, cotangent))
    return (produced, grads[0], grads[1], grads[2], grads[3], grads[4], grads[5], grads[6], grads[7])
```

```python
from functools import partial

import jax
import jax.numpy as jnp
from jax import lax
from jax.sharding import PartitionSpec as P

BLOCK = 128


EPS = 1e-05
HIGH = lax.Precision.HIGHEST


def shifted(value, axis, steps):
    count = lax.axis_size(axis)
    leading, last = (max(0, -steps), min(count, count - steps))
    return lax.ppermute(value, axis, [(source, source + steps) for source in range(leading, last)])


def indicator(labels, vocab, kind):
    return (labels[:, None] == jnp.arange(vocab, dtype=jnp.int32)[None, :]).astype(kind)


def running(value):
    items = value.shape[1]
    lower = jnp.tril(jnp.ones((items, items), jnp.float32))
    return jnp.einsum("ts,csh->cth", lower, value, precision=HIGH)


def total_over_devices(arrays):
    axes = ("seq", "batch")
    parts = lax.axis_size(axes)
    lanes = 128
    rows = []
    for array in arrays:
        flat = array.reshape(-1)
        rows.append(jnp.pad(flat, (0, -flat.size % lanes)).reshape(-1, lanes))
    counts = [piece.shape[0] for piece in rows]
    stacked = jnp.concatenate(rows)
    share = -(-stacked.shape[0] // (8 * parts)) * 8
    stacked = jnp.pad(stacked, ((0, share * parts - stacked.shape[0]), (0, 0)))
    pieces = lax.all_to_all(
        stacked.reshape(parts, share, lanes), axes, split_axis=0, concat_axis=0, tiled=True
    )
    mine = jnp.sum(pieces, axis=0)
    whole = lax.all_to_all(
        jnp.broadcast_to(mine[None], (parts, share, lanes)),
        axes,
        split_axis=0,
        concat_axis=0,
        tiled=True,
    ).reshape(parts * share, lanes)
    results = []
    start = 0
    for array, count in zip(arrays, counts):
        flat = whole[start : start + count].reshape(-1)
        results.append(flat[: array.size].reshape(array.shape))
        start += count
    return results


def prepare(raw_rows, step_rows, decay_log, conv_weight, conv_bias, inner, heads):
    width = conv_weight.shape[0]
    tokens = raw_rows.shape[0] - width + 1
    state = (raw_rows.shape[1] - inner) // 2
    convolved = conv_bias[None, :] + conv_weight[0][None, :] * raw_rows[0:tokens]
    for offset in range(1, width):
        convolved = convolved + conv_weight[offset][None, :] * raw_rows[offset : offset + tokens]
    active = jax.nn.silu(convolved)
    values = active[:, :inner].astype(jnp.bfloat16).reshape(tokens, heads, inner // heads)
    write_keys = active[:, inner : inner + state].astype(jnp.bfloat16)
    read_keys = active[:, inner + state :].astype(jnp.bfloat16)
    steps = jax.nn.softplus(step_rows)
    log_decay = -jnp.exp(decay_log)[None, :] * steps
    return (values, write_keys, read_keys, steps, log_decay)


def group_states(values, write_keys, steps, log_decay):
    tokens, heads, head = values.shape
    count = tokens // BLOCK
    cum = running(log_decay.reshape(count, BLOCK, heads))
    factor = jnp.exp(cum[:, -1:, :] - cum) * steps.reshape(count, BLOCK, heads)
    weighted = (values.reshape(count, BLOCK, heads, head) * factor[..., None]).astype(jnp.bfloat16)
    return jnp.einsum(
        "cshp,csn->chpn",
        weighted,
        write_keys.reshape(count, BLOCK, -1),
        preferred_element_type=jnp.float32,
    )


def local_states(pieces, log_decay):
    count = pieces.shape[0]
    block_total = jnp.sum(log_decay.reshape(count, BLOCK, -1), axis=1)

    def advance(carried, item):
        piece, total = item
        return (jnp.exp(total)[:, None, None] * carried + piece, carried)

    final, entering = lax.scan(advance, jnp.zeros_like(pieces[0]), (pieces, block_total))
    return (entering, final, jnp.sum(block_total, axis=0))


def mixer_output(
    values,
    write_keys,
    read_keys,
    steps,
    log_decay,
    entering,
    carried,
    gate_rows,
    skip_gain,
    norm_gain,
):
    tokens, heads, head = values.shape
    count = tokens // BLOCK
    cum = running(log_decay.reshape(count, BLOCK, heads))
    block_total = cum[:, -1, :]
    before = running(block_total[None])[0] - block_total
    states = entering + jnp.exp(before)[:, :, None, None] * carried[None]
    writes = write_keys.reshape(count, BLOCK, -1)
    reads = read_keys.reshape(count, BLOCK, -1)
    scores = jnp.einsum("ctn,csn->cts", reads, writes, preferred_element_type=jnp.float32)
    lower = (
        lax.broadcasted_iota(jnp.int32, (BLOCK, BLOCK), 0)
        >= lax.broadcasted_iota(jnp.int32, (BLOCK, BLOCK), 1)
    )[None, None]
    track = jnp.transpose(cum, (0, 2, 1))
    power = track[:, :, :, None] - track[:, :, None, :]
    fade = jnp.where(lower, jnp.exp(jnp.where(lower, power, 0.0)), 0.0)
    widths = jnp.transpose(steps.reshape(count, BLOCK, heads), (0, 2, 1))
    mixing = (scores[:, None] * fade * widths[:, :, None, :]).astype(jnp.bfloat16)
    blocked = values.reshape(count, BLOCK, heads, head)
    within = jnp.einsum("chts,cshp->cthp", mixing, blocked, preferred_element_type=jnp.float32)
    across = jnp.exp(cum)[..., None] * jnp.einsum(
        "ctn,chpn->cthp", reads, states.astype(jnp.bfloat16), preferred_element_type=jnp.float32
    )
    mixed = within + across + skip_gain[None, None, :, None] * blocked
    gated = mixed.reshape(tokens, heads * head) * jax.nn.silu(gate_rows)
    scale = lax.rsqrt(jnp.mean(gated * gated, axis=1, keepdims=True) + EPS)
    return (gated * scale * norm_gain[None, :]).astype(jnp.bfloat16)


def carry_weights(logs, backward):
    parts = logs.shape[1]
    inclusive = running(logs.T[None])[0].T
    exclusive = inclusive - logs
    rows = lax.broadcasted_iota(jnp.int32, (parts, parts), 0)
    cols = lax.broadcasted_iota(jnp.int32, (parts, parts), 1)
    if backward:
        keep = (cols > rows)[None]
        power = exclusive[:, None, :] - inclusive[:, :, None]
    else:
        keep = (cols < rows)[None]
        power = exclusive[:, :, None] - inclusive[:, None, :]
    return jnp.where(keep, jnp.exp(jnp.where(keep, power, 0.0)), 0.0)


def settle_forward(pieces):
    states_in, totals_in = pieces
    weights = carry_weights(totals_in[:, :, 0], False)
    settled = jnp.einsum("hij,hjw->hiw", weights, states_in, precision=HIGH)
    return lax.all_to_all(settled, "seq", split_axis=1, concat_axis=1, tiled=True)


def settle_backward(pieces):
    states_in, totals_in = pieces
    weights = carry_weights(totals_in[:, :, 0], True)
    settled = jnp.einsum("hij,hjw->hiw", weights, states_in, precision=HIGH)
    return lax.all_to_all(settled, "seq", split_axis=1, concat_axis=1, tiled=True)


def local(
    token_ids,
    input_table,
    gate_table,
    step_table,
    decay_log,
    conv_weight,
    conv_bias,
    skip_gain,
    norm_gain,
    cotangent,
):
    labels = token_ids[0]
    tokens = labels.shape[0]
    width = conv_weight.shape[0]
    vocab = input_table.shape[0]
    inner = gate_table.shape[1]
    heads = step_table.shape[1]
    rim = shifted(labels[tokens - width + 1 :] + 1, "seq", 1) - 1
    extended = jnp.concatenate([rim, labels])
    wide_hot = indicator(extended, vocab, jnp.bfloat16)
    own_hot = wide_hot[width - 1 :]
    raw_rows = jnp.dot(wide_hot, input_table, preferred_element_type=jnp.float32)
    gate_rows = jnp.dot(own_hot, gate_table, preferred_element_type=jnp.float32)
    step_rows = jnp.dot(own_hot.astype(jnp.float32), step_table, precision=HIGH)
    features, pull_prepare = jax.vjp(
        partial(prepare, inner=inner, heads=heads),
        raw_rows,
        step_rows,
        decay_log,
        conv_weight,
        conv_bias,
    )
    values, write_keys, read_keys, steps, log_decay = features
    pieces, pull_groups = jax.vjp(group_states, values, write_keys, steps, log_decay)
    (entering, final, total), pull_local = jax.vjp(local_states, pieces, log_decay)
    flat = final.reshape(heads, -1)
    parts = lax.axis_size("seq")
    span = flat.shape[1] // parts
    totals = jnp.broadcast_to(total[:, None, None], (heads, parts, 1))
    carried = settle_forward(
        (
            lax.all_to_all(
                flat.reshape(heads, parts, span), "seq", split_axis=1, concat_axis=1, tiled=True
            ),
            lax.all_to_all(totals, "seq", split_axis=1, concat_axis=1, tiled=True),
        )
    ).reshape(final.shape)
    layer_out, pull_out = jax.vjp(
        mixer_output,
        values,
        write_keys,
        read_keys,
        steps,
        log_decay,
        entering,
        carried,
        gate_rows,
        skip_gain,
        norm_gain,
    )
    d_values, d_write, d_read, d_steps, d_log, d_entering, d_carried, d_gate, d_skip, d_norm = (
        pull_out(cotangent[0])
    )
    back_flat = d_carried.reshape(heads, -1)
    later = settle_backward(
        (
            lax.all_to_all(
                back_flat.reshape(heads, parts, span),
                "seq",
                split_axis=1,
                concat_axis=1,
                tiled=True,
            ),
            lax.all_to_all(totals, "seq", split_axis=1, concat_axis=1, tiled=True),
        )
    ).reshape(final.shape)
    d_total = jnp.exp(total) * jnp.sum(later * carried, axis=(1, 2))
    d_pieces, d_log_local = pull_local((d_entering, later, d_total))
    d_values_state, d_write_state, d_steps_state, d_log_state = pull_groups(d_pieces)
    d_raw, d_step_rows, d_decay, d_taps, d_shift = pull_prepare(
        (
            d_values + d_values_state,
            d_write + d_write_state,
            d_read,
            d_steps + d_steps_state,
            d_log + d_log_state + d_log_local,
        )
    )
    wide_float = wide_hot.astype(jnp.float32)
    own_float = wide_float[width - 1 :]
    sums = total_over_devices(
        (
            jnp.dot(wide_float.T, d_raw, precision=lax.Precision.HIGH),
            jnp.dot(own_float.T, d_gate, precision=lax.Precision.HIGH),
            jnp.dot(own_float.T, d_step_rows, precision=lax.Precision.HIGH),
            d_decay,
            d_taps,
            d_shift,
            d_skip,
            d_norm,
        )
    )
    return (layer_out[None], sums[0], sums[1], sums[2], sums[3], sums[4], sums[5], sums[6], sums[7])


def solution(mesh):
    return jax.shard_map(
        local,
        mesh=mesh,
        in_specs=(
            P("batch", "seq"),
            P(),
            P(),
            P(),
            P(),
            P(),
            P(),
            P(),
            P(),
            P("batch", "seq", None),
        ),
        out_specs=(P("batch", "seq", None), P(), P(), P(), P(), P(), P(), P(), P()),
        check_vma=False,
    )
```

```python
import jax
import jax.numpy as jnp
from jax import lax
from jax.sharding import PartitionSpec as P

BLOCK = 128


EPS = 1e-05
HIGH = lax.Precision.HIGHEST
THREE = lax.Precision.HIGH


def total_over_devices(arrays):
    axes = ("seq", "batch")
    parts = lax.axis_size(axes)
    lanes = 128
    rows = []
    for array in arrays:
        flat = array.reshape(-1)
        rows.append(jnp.pad(flat, (0, -flat.size % lanes)).reshape(-1, lanes))
    counts = [piece.shape[0] for piece in rows]
    stacked = jnp.concatenate(rows)
    share = -(-stacked.shape[0] // (8 * parts)) * 8
    stacked = jnp.pad(stacked, ((0, share * parts - stacked.shape[0]), (0, 0)))
    pieces = lax.all_to_all(
        stacked.reshape(parts, share, lanes), axes, split_axis=0, concat_axis=0, tiled=True
    )
    mine = jnp.sum(pieces, axis=0)
    whole = lax.all_to_all(
        jnp.broadcast_to(mine[None], (parts, share, lanes)),
        axes,
        split_axis=0,
        concat_axis=0,
        tiled=True,
    ).reshape(parts * share, lanes)
    results = []
    start = 0
    for array, count in zip(arrays, counts):
        flat = whole[start : start + count].reshape(-1)
        results.append(flat[: array.size].reshape(array.shape))
        start += count
    return results


def indicator(labels, vocab):
    return (jnp.arange(vocab, dtype=jnp.int32)[:, None] == labels[None, :]).astype(jnp.float32)


def decays(step_rows, decay_log):
    steps = jax.nn.softplus(step_rows)
    return (steps, -jnp.exp(decay_log)[:, None] * steps)


def activate(convolved, inner):
    active = jax.nn.silu(convolved)
    state = (convolved.shape[0] - inner) // 2
    return (
        active[:inner].astype(jnp.bfloat16),
        active[inner : inner + state].astype(jnp.bfloat16),
        active[inner + state :].astype(jnp.bfloat16),
    )


def blocks(value):
    return [value[:, at : at + BLOCK] for at in range(0, value.shape[1], BLOCK)]


def running(logs):
    lower = jnp.tril(jnp.ones((BLOCK, BLOCK), jnp.float32))
    return jnp.einsum("hs,ts->ht", logs, lower, precision=HIGH)


def by_head(rows, heads):
    return rows.reshape(heads, rows.shape[0] // heads, rows.shape[1])


def local_states(values, write_keys, steps, log_decay):
    heads = steps.shape[0]
    state = None
    entering = []
    total = jnp.zeros((heads,), jnp.float32)
    for vals, writes, widths, logs in zip(*map(blocks, (values, write_keys, steps, log_decay))):
        cum = running(logs)
        last = cum[:, -1:]
        factor = jnp.exp(last - cum) * widths
        weighted = (by_head(vals, heads) * factor[:, None, :]).astype(jnp.bfloat16)
        piece = jnp.einsum(
            "cs,ns->cn",
            weighted.reshape(vals.shape),
            writes,
            preferred_element_type=jnp.float32,
        )
        piece = by_head(piece, heads)
        if state is None:
            state = piece
        else:
            entering.append(state)
            state = jnp.exp(last)[:, :, None] * state + piece
        total = total + last[:, 0]
    return (tuple(entering), state, total)


def mixed_rows(
    values, write_keys, read_keys, steps, log_decay, entering, carried, skip_gain
):
    heads = steps.shape[0]
    source = lax.broadcasted_iota(jnp.int32, (BLOCK, BLOCK), 0)
    target = lax.broadcasted_iota(jnp.int32, (BLOCK, BLOCK), 1)
    keep = (source <= target)[None]
    before = jnp.zeros((heads,), jnp.float32)
    parts = []
    for number, (vals, writes, reads, widths, logs) in enumerate(
        zip(*map(blocks, (values, write_keys, read_keys, steps, log_decay)))
    ):
        cum = running(logs)
        states = jnp.exp(before)[:, None, None] * carried
        if number:
            states = entering[number - 1] + states
        scores = jnp.einsum("ns,nt->st", writes, reads, preferred_element_type=jnp.float32)
        power = cum[:, None, :] - cum[:, :, None]
        fade = jnp.where(keep, jnp.exp(jnp.where(keep, power, 0.0)), 0.0)
        mixing = (scores[None] * fade * widths[:, :, None]).astype(jnp.bfloat16)
        blocked = by_head(vals, heads)
        within = jnp.einsum("hps,hst->hpt", blocked, mixing, preferred_element_type=jnp.float32)
        across = jnp.einsum(
            "cn,nt->ct",
            states.astype(jnp.bfloat16).reshape(vals.shape[0], -1),
            reads,
            preferred_element_type=jnp.float32,
        )
        parts.append(
            within
            + jnp.exp(cum)[:, None, :] * by_head(across, heads)
            + skip_gain[:, None, None] * blocked
        )
        before = before + cum[:, -1]
    return jnp.concatenate(parts, axis=2).reshape(values.shape)


def normalised(mixed, gate_rows, norm_gain):
    gated = mixed * jax.nn.silu(gate_rows)
    scale = lax.rsqrt(jnp.mean(gated * gated, axis=0, keepdims=True) + EPS)
    return (gated * scale * norm_gain[:, None]).astype(jnp.bfloat16)


def carry_weights(logs, backward):
    parts = logs.shape[0]
    lower = jnp.tril(jnp.ones((parts, parts), jnp.float32))
    inclusive = jnp.einsum("ij,jr->ir", lower, logs, precision=HIGH)
    exclusive = inclusive - logs
    rows = lax.broadcasted_iota(jnp.int32, (parts, parts), 0)
    cols = lax.broadcasted_iota(jnp.int32, (parts, parts), 1)
    if backward:
        keep = (cols > rows)[:, :, None]
        power = exclusive[None, :, :] - inclusive[:, None, :]
    else:
        keep = (cols < rows)[:, :, None]
        power = exclusive[:, None, :] - inclusive[None, :, :]
    return jnp.where(keep, jnp.exp(jnp.where(keep, power, 0.0)), 0.0)


def settle(state, row_logs, backward):
    heads, head, width = state.shape
    parts, span = row_logs.shape
    pieces = lax.all_to_all(
        state.reshape(parts, span, width), "seq", split_axis=0, concat_axis=0, tiled=True
    )
    weights = carry_weights(row_logs, backward)
    settled = jnp.sum(weights[:, :, :, None] * pieces[None], axis=1)
    return lax.all_to_all(settled, "seq", split_axis=0, concat_axis=0, tiled=True).reshape(
        state.shape
    )


def local(
    token_ids,
    input_table,
    gate_table,
    step_table,
    decay_log,
    conv_weight,
    conv_bias,
    skip_gain,
    norm_gain,
    cotangent,
):
    labels = token_ids[0]
    tokens = labels.shape[0]
    width = conv_weight.shape[0]
    vocab, channels = input_table.shape
    inner = gate_table.shape[1]
    heads = step_table.shape[1]
    head = inner // heads
    parts = lax.axis_size("seq")
    index = lax.axis_index("seq")
    own_hot = indicator(labels, vocab)
    step_rows = jnp.einsum("vh,vt->ht", step_table, own_hot, precision=HIGH)
    (steps, log_decay), pull_decays = jax.vjp(decays, step_rows, decay_log)
    rim = width - 1
    message = jnp.concatenate(
        [(labels[tokens - rim :] + 1).astype(jnp.float32), jnp.sum(log_decay, axis=1)]
    )
    heard = lax.all_to_all(
        jnp.broadcast_to(message[None], (parts, rim + heads)),
        "seq",
        split_axis=0,
        concat_axis=0,
        tiled=True,
    )
    previous = (jnp.arange(parts) == index - 1)[:, None]
    edge = jnp.sum(jnp.where(previous, heard[:, :rim], 0.0), axis=0).astype(jnp.int32) - 1
    span = inner // parts
    owner = (index * span + jnp.arange(span, dtype=jnp.int32)) // head
    row_logs = jnp.einsum("jh,hr->jr", heard[:, rim:], indicator(owner, heads), precision=HIGH)

    extended = jnp.concatenate([edge, labels])
    hot = jnp.concatenate([indicator(extended[k : k + tokens], vocab) for k in range(width)])
    table = input_table.astype(jnp.float32)
    tapped = (conv_weight[:, None, :] * table[None]).reshape(width * vocab, channels)
    convolved = jnp.einsum("kc,kt->ct", tapped, hot, precision=HIGH) + conv_bias[:, None]
    gate_rows = jnp.einsum(
        "vc,vt->ct", gate_table, own_hot.astype(jnp.bfloat16), preferred_element_type=jnp.float32
    )
    (values, write_keys, read_keys), pull_activate = jax.vjp(
        lambda rows: activate(rows, inner), convolved
    )
    (entering, final, total), pull_local = jax.vjp(
        local_states, values, write_keys, steps, log_decay
    )
    carried = settle(final, row_logs, False)
    mixed, pull_mixed = jax.vjp(
        mixed_rows,
        values,
        write_keys,
        read_keys,
        steps,
        log_decay,
        entering,
        carried,
        skip_gain,
    )
    layer_out, pull_out = jax.vjp(normalised, mixed, gate_rows, norm_gain)
    d_mixed, d_gate, d_norm = pull_out(cotangent[0].T)
    d_values, d_write, d_read, d_steps, d_log, d_entering, d_carried, d_skip = pull_mixed(d_mixed)
    later = settle(d_carried, row_logs, True)
    d_total = jnp.exp(total) * jnp.sum(later * carried, axis=(1, 2))
    d_values_state, d_write_state, d_steps_state, d_log_state = pull_local(
        (d_entering, later, d_total)
    )
    (d_convolved,) = pull_activate(
        (d_values + d_values_state, d_write + d_write_state, d_read)
    )
    d_step_rows, d_decay = pull_decays((d_steps + d_steps_state, d_log + d_log_state))
    spread = jnp.einsum("kt,ct->kc", hot, d_convolved, precision=THREE)
    spread = spread.reshape(width, vocab, channels)
    sums = total_over_devices(
        (
            jnp.sum(conv_weight[:, None, :] * spread, axis=0),
            jnp.einsum("vt,ct->vc", own_hot, d_gate, precision=THREE),
            jnp.einsum("vt,ht->vh", own_hot, d_step_rows, precision=HIGH),
            d_decay,
            jnp.sum(table[None] * spread, axis=1),
            jnp.sum(spread[width - 1], axis=0),
            d_skip,
            d_norm,
        )
    )
    return (layer_out.T[None], *sums)


def solution(mesh):
    return jax.shard_map(
        local,
        mesh=mesh,
        in_specs=(
            P("batch", "seq"),
            P(),
            P(),
            P(),
            P(),
            P(),
            P(),
            P(),
            P(),
            P("batch", "seq", None),
        ),
        out_specs=(P("batch", "seq", None), P(), P(), P(), P(), P(), P(), P(), P()),
        check_vma=False,
    )
```

```python
import jax
import jax.numpy as jnp
from jax import lax
from jax.sharding import PartitionSpec as P

BLOCK = 128


EPS = 1e-05
HIGH = lax.Precision.HIGHEST
THREE = lax.Precision.HIGH


def total_over_devices(arrays):
    axes = ("seq", "batch")
    parts = lax.axis_size(axes)
    lanes = 128
    rows = []
    for array in arrays:
        flat = array.reshape(-1)
        rows.append(jnp.pad(flat, (0, -flat.size % lanes)).reshape(-1, lanes))
    counts = [piece.shape[0] for piece in rows]
    stacked = jnp.concatenate(rows)
    share = -(-stacked.shape[0] // (8 * parts)) * 8
    stacked = jnp.pad(stacked, ((0, share * parts - stacked.shape[0]), (0, 0)))
    pieces = lax.all_to_all(
        stacked.reshape(parts, share, lanes), axes, split_axis=0, concat_axis=0, tiled=True
    )
    mine = jnp.sum(pieces, axis=0)
    whole = lax.all_to_all(
        jnp.broadcast_to(mine[None], (parts, share, lanes)),
        axes,
        split_axis=0,
        concat_axis=0,
        tiled=True,
    ).reshape(parts * share, lanes)
    results = []
    start = 0
    for array, count in zip(arrays, counts):
        flat = whole[start : start + count].reshape(-1)
        results.append(flat[: array.size].reshape(array.shape))
        start += count
    return results


def indicator(labels, vocab):
    return (jnp.arange(vocab, dtype=jnp.int32)[:, None] == labels[None, :]).astype(jnp.float32)


def decays(step_rows, decay_log):
    steps = jax.nn.softplus(step_rows)
    return (steps, -jnp.exp(decay_log)[:, None] * steps)


def activate(convolved, inner):
    active = jax.nn.silu(convolved)
    state = (convolved.shape[0] - inner) // 2
    return (
        active[:inner].astype(jnp.bfloat16),
        active[inner : inner + state].astype(jnp.bfloat16),
        active[inner + state :].astype(jnp.bfloat16),
    )


def blocks(value):
    return [value[:, at : at + BLOCK] for at in range(0, value.shape[1], BLOCK)]


def running(logs):
    lower = jnp.tril(jnp.ones((BLOCK, BLOCK), jnp.float32))
    return jnp.einsum("hs,ts->ht", logs, lower, precision=HIGH)


def by_head(rows, heads):
    return rows.reshape(heads, rows.shape[0] // heads, rows.shape[1])


def local_states(values, write_keys, steps, log_decay):
    heads = steps.shape[0]
    state = None
    entering = []
    total = jnp.zeros((heads,), jnp.float32)
    for vals, writes, widths, logs in zip(*map(blocks, (values, write_keys, steps, log_decay))):
        cum = running(logs)
        last = cum[:, -1:]
        factor = jnp.exp(last - cum) * widths
        weighted = (by_head(vals, heads) * factor[:, None, :]).astype(jnp.bfloat16)
        piece = jnp.einsum(
            "cs,ns->cn",
            weighted.reshape(vals.shape),
            writes,
            preferred_element_type=jnp.float32,
        )
        piece = by_head(piece, heads)
        if state is None:
            state = piece
        else:
            entering.append(state)
            state = jnp.exp(last)[:, :, None] * state + piece
        total = total + last[:, 0]
    return (tuple(entering), state, total)


def mixed_rows(
    values, write_keys, read_keys, steps, log_decay, entering, carried, skip_gain
):
    heads = steps.shape[0]
    source = lax.broadcasted_iota(jnp.int32, (BLOCK, BLOCK), 0)
    target = lax.broadcasted_iota(jnp.int32, (BLOCK, BLOCK), 1)
    keep = (source <= target)[None]
    before = jnp.zeros((heads,), jnp.float32)
    parts = []
    for number, (vals, writes, reads, widths, logs) in enumerate(
        zip(*map(blocks, (values, write_keys, read_keys, steps, log_decay)))
    ):
        cum = running(logs)
        states = jnp.exp(before)[:, None, None] * carried
        if number:
            states = entering[number - 1] + states
        scores = jnp.einsum("ns,nt->st", writes, reads, preferred_element_type=jnp.float32)
        power = cum[:, None, :] - cum[:, :, None]
        fade = jnp.where(keep, jnp.exp(jnp.where(keep, power, 0.0)), 0.0)
        mixing = (scores[None] * fade * widths[:, :, None]).astype(jnp.bfloat16)
        blocked = by_head(vals, heads)
        within = jnp.einsum("hps,hst->hpt", blocked, mixing, preferred_element_type=jnp.float32)
        across = jnp.einsum(
            "cn,nt->ct",
            states.astype(jnp.bfloat16).reshape(vals.shape[0], -1),
            reads,
            preferred_element_type=jnp.float32,
        )
        parts.append(
            within
            + jnp.exp(cum)[:, None, :] * by_head(across, heads)
            + skip_gain[:, None, None] * blocked
        )
        before = before + cum[:, -1]
    return jnp.concatenate(parts, axis=2).reshape(values.shape)


def normalised(mixed, gate_rows, norm_gain):
    gated = mixed * jax.nn.silu(gate_rows)
    scale = lax.rsqrt(jnp.mean(gated * gated, axis=0, keepdims=True) + EPS)
    return (gated * scale * norm_gain[:, None]).astype(jnp.bfloat16)


def earlier_state(hot, fading, tapped, conv_bias, inner):
    heads = fading.shape[0]
    used = (inner + tapped.shape[1]) // 2
    tapped = tapped[:, :used]
    shift = conv_bias[:used, None]

    def of_group(hot, fading):
        rows = jnp.einsum("kc,kt->ct", tapped, hot, precision=THREE) + shift
        active = jax.nn.silu(rows)
        vals = active[:inner].astype(jnp.bfloat16)
        writes = active[inner:].astype(jnp.bfloat16)
        weighted = (by_head(vals, heads) * fading[:, None, :]).astype(jnp.bfloat16)
        return jnp.einsum(
            "cs,ns->cn", weighted.reshape(vals.shape), writes, preferred_element_type=jnp.float32
        )

    tokens = hot.shape[1]
    group = 2048
    if tokens <= group or tokens % group:
        return by_head(of_group(hot, fading), heads)

    def grouped(value):
        return jnp.moveaxis(value.reshape(value.shape[0], -1, group), 1, 0)

    def add(state, item):
        return (state + of_group(*item), None)

    start = jnp.zeros((inner, used - inner), jnp.float32)
    return by_head(lax.scan(add, start, (grouped(hot), grouped(fading)))[0], heads)


def carry_weights(logs):
    parts = logs.shape[0]
    lower = jnp.tril(jnp.ones((parts, parts), jnp.float32))
    inclusive = jnp.einsum("ij,jr->ir", lower, logs, precision=HIGH)
    exclusive = inclusive - logs
    rows = lax.broadcasted_iota(jnp.int32, (parts, parts), 0)
    cols = lax.broadcasted_iota(jnp.int32, (parts, parts), 1)
    keep = (cols > rows)[:, :, None]
    power = exclusive[None, :, :] - inclusive[:, None, :]
    return jnp.where(keep, jnp.exp(jnp.where(keep, power, 0.0)), 0.0)


def settle(state, row_logs):
    width = state.shape[2]
    parts, span = row_logs.shape
    pieces = lax.all_to_all(
        state.reshape(parts, span, width), "seq", split_axis=0, concat_axis=0, tiled=True
    )
    settled = jnp.sum(carry_weights(row_logs)[:, :, :, None] * pieces[None], axis=1)
    return lax.all_to_all(settled, "seq", split_axis=0, concat_axis=0, tiled=True).reshape(
        state.shape
    )


def local(
    token_ids,
    input_table,
    gate_table,
    step_table,
    decay_log,
    conv_weight,
    conv_bias,
    skip_gain,
    norm_gain,
    cotangent,
):
    labels = token_ids[0]
    tokens = labels.shape[0]
    width = conv_weight.shape[0]
    vocab, channels = input_table.shape
    inner = gate_table.shape[1]
    heads = step_table.shape[1]
    head = inner // heads
    parts = lax.axis_size("seq")
    index = lax.axis_index("seq")
    own_hot = indicator(labels, vocab)
    step_rows = jnp.einsum("vh,vt->ht", step_table, own_hot, precision=HIGH)
    (steps, log_decay), pull_decays = jax.vjp(decays, step_rows, decay_log)
    rim = width - 1
    heard = lax.all_to_all(
        jnp.broadcast_to(labels[None], (parts, tokens)),
        "seq",
        split_axis=0,
        concat_axis=0,
        tiled=True,
    )
    numbers = jnp.arange(parts, dtype=jnp.int32)
    previous = (numbers == index - 1)[:, None]
    edge = jnp.sum(jnp.where(previous, heard[:, tokens - rim :] + 1, 0), axis=0) - 1
    whole = heard.reshape(parts * tokens)
    padded = jnp.concatenate([jnp.full((rim,), -1, jnp.int32), whole])
    whole_hot = jnp.concatenate(
        [indicator(padded[k : k + parts * tokens], vocab) for k in range(width)]
    )
    whole_steps, whole_logs = decays(
        jnp.einsum("vh,vt->ht", step_table, whole_hot[rim * vocab :], precision=HIGH), decay_log
    )
    lower = jnp.tril(jnp.ones((tokens, tokens), jnp.float32))
    cum = jnp.einsum(
        "hjs,ts->hjt", whole_logs.reshape(heads, parts, tokens), lower, precision=HIGH
    )
    totals = cum[:, :, -1]
    between = (numbers[None, :] > numbers[:, None]) & (numbers[None, :] < index)
    tail = jnp.einsum("jm,hm->hj", between.astype(jnp.float32), totals, precision=HIGH)
    fading = jnp.exp((totals + tail)[:, :, None] - cum) * (numbers < index)[None, :, None]
    fading = fading.reshape(heads, parts * tokens) * whole_steps
    span = inner // parts
    owner = (index * span + jnp.arange(span, dtype=jnp.int32)) // head
    row_logs = jnp.einsum("hj,hr->jr", totals, indicator(owner, heads), precision=HIGH)

    extended = jnp.concatenate([edge, labels])
    hot = jnp.concatenate([indicator(extended[k : k + tokens], vocab) for k in range(width)])
    table = input_table.astype(jnp.float32)
    tapped = (conv_weight[:, None, :] * table[None]).reshape(width * vocab, channels)
    convolved = jnp.einsum("kc,kt->ct", tapped, hot, precision=HIGH) + conv_bias[:, None]
    gate_rows = jnp.einsum(
        "vc,vt->ct", gate_table, own_hot.astype(jnp.bfloat16), preferred_element_type=jnp.float32
    )
    (values, write_keys, read_keys), pull_activate = jax.vjp(
        lambda rows: activate(rows, inner), convolved
    )
    (entering, _, total), pull_local = jax.vjp(
        local_states, values, write_keys, steps, log_decay
    )
    carried = earlier_state(whole_hot, fading, tapped, conv_bias, inner)
    mixed, pull_mixed = jax.vjp(
        mixed_rows,
        values,
        write_keys,
        read_keys,
        steps,
        log_decay,
        entering,
        carried,
        skip_gain,
    )
    layer_out, pull_out = jax.vjp(normalised, mixed, gate_rows, norm_gain)
    d_mixed, d_gate, d_norm = pull_out(cotangent[0].T)
    d_values, d_write, d_read, d_steps, d_log, d_entering, d_carried, d_skip = pull_mixed(d_mixed)
    later = settle(d_carried, row_logs)
    d_total = jnp.exp(total) * jnp.sum(later * carried, axis=(1, 2))
    d_values_state, d_write_state, d_steps_state, d_log_state = pull_local(
        (d_entering, later, d_total)
    )
    (d_convolved,) = pull_activate(
        (d_values + d_values_state, d_write + d_write_state, d_read)
    )
    d_step_rows, d_decay = pull_decays((d_steps + d_steps_state, d_log + d_log_state))
    spread = jnp.einsum("kt,ct->kc", hot, d_convolved, precision=THREE)
    spread = spread.reshape(width, vocab, channels)
    sums = total_over_devices(
        (
            jnp.sum(conv_weight[:, None, :] * spread, axis=0),
            jnp.einsum("vt,ct->vc", own_hot, d_gate, precision=THREE),
            jnp.einsum("vt,ht->vh", own_hot, d_step_rows, precision=HIGH),
            d_decay,
            jnp.sum(table[None] * spread, axis=1),
            jnp.sum(spread[width - 1], axis=0),
            d_skip,
            d_norm,
        )
    )
    return (layer_out.T[None], *sums)


def solution(mesh):
    return jax.shard_map(
        local,
        mesh=mesh,
        in_specs=(
            P("batch", "seq"),
            P(),
            P(),
            P(),
            P(),
            P(),
            P(),
            P(),
            P(),
            P("batch", "seq", None),
        ),
        out_specs=(P("batch", "seq", None), P(), P(), P(), P(), P(), P(), P(), P()),
        check_vma=False,
    )
```

```python
import jax
import jax.numpy as jnp
from jax import lax
from jax.sharding import PartitionSpec as P

BLOCK = 128


EPS = 1e-05
HIGH = lax.Precision.HIGHEST
THREE = lax.Precision.HIGH


def total_over_devices(arrays):
    axes = ("seq", "batch")
    parts = lax.axis_size(axes)
    lanes = 128
    rows = []
    for array in arrays:
        flat = array.reshape(-1)
        rows.append(jnp.pad(flat, (0, -flat.size % lanes)).reshape(-1, lanes))
    counts = [piece.shape[0] for piece in rows]
    stacked = jnp.concatenate(rows)
    share = -(-stacked.shape[0] // (8 * parts)) * 8
    stacked = jnp.pad(stacked, ((0, share * parts - stacked.shape[0]), (0, 0)))
    pieces = lax.all_to_all(
        stacked.reshape(parts, share, lanes), axes, split_axis=0, concat_axis=0, tiled=True
    )
    mine = jnp.sum(pieces, axis=0)
    whole = lax.all_to_all(
        jnp.broadcast_to(mine[None], (parts, share, lanes)),
        axes,
        split_axis=0,
        concat_axis=0,
        tiled=True,
    ).reshape(parts * share, lanes)
    results = []
    start = 0
    for array, count in zip(arrays, counts):
        flat = whole[start : start + count].reshape(-1)
        results.append(flat[: array.size].reshape(array.shape))
        start += count
    return results


def indicator(labels, vocab):
    return (jnp.arange(vocab, dtype=jnp.int32)[:, None] == labels[None, :]).astype(jnp.float32)


def decays(step_rows, decay_log):
    steps = jax.nn.softplus(step_rows)
    return (steps, -jnp.exp(decay_log)[:, None] * steps)


def activate(convolved, inner):
    active = jax.nn.silu(convolved)
    state = (convolved.shape[0] - inner) // 2
    return (
        active[:inner].astype(jnp.bfloat16),
        active[inner : inner + state].astype(jnp.bfloat16),
        active[inner + state :].astype(jnp.bfloat16),
    )


def blocks(value):
    return [value[:, at : at + BLOCK] for at in range(0, value.shape[1], BLOCK)]


def running(logs):
    lower = jnp.tril(jnp.ones((BLOCK, BLOCK), jnp.float32))
    return jnp.einsum("hs,ts->ht", logs, lower, precision=HIGH)


def by_head(rows, heads):
    return rows.reshape(heads, rows.shape[0] // heads, rows.shape[1])


def local_states(values, write_keys, steps, log_decay):
    heads = steps.shape[0]
    state = None
    entering = []
    total = jnp.zeros((heads,), jnp.float32)
    for vals, writes, widths, logs in zip(*map(blocks, (values, write_keys, steps, log_decay))):
        cum = running(logs)
        last = cum[:, -1:]
        factor = jnp.exp(last - cum) * widths
        weighted = (by_head(vals, heads) * factor[:, None, :]).astype(jnp.bfloat16)
        piece = jnp.einsum(
            "cs,ns->cn",
            weighted.reshape(vals.shape),
            writes,
            preferred_element_type=jnp.float32,
        )
        piece = by_head(piece, heads)
        if state is None:
            state = piece
        else:
            entering.append(state)
            state = jnp.exp(last)[:, :, None] * state + piece
        total = total + last[:, 0]
    return (tuple(entering), state, total)


def mixed_rows(
    values, write_keys, read_keys, steps, log_decay, entering, carried, skip_gain
):
    heads = steps.shape[0]
    source = lax.broadcasted_iota(jnp.int32, (BLOCK, BLOCK), 0)
    target = lax.broadcasted_iota(jnp.int32, (BLOCK, BLOCK), 1)
    keep = (source <= target)[None]
    before = jnp.zeros((heads,), jnp.float32)
    parts = []
    for number, (vals, writes, reads, widths, logs) in enumerate(
        zip(*map(blocks, (values, write_keys, read_keys, steps, log_decay)))
    ):
        cum = running(logs)
        states = jnp.exp(before)[:, None, None] * carried
        if number:
            states = entering[number - 1] + states
        scores = jnp.einsum("ns,nt->st", writes, reads, preferred_element_type=jnp.float32)
        power = cum[:, None, :] - cum[:, :, None]
        fade = jnp.where(keep, jnp.exp(jnp.where(keep, power, 0.0)), 0.0)
        mixing = (scores[None] * fade * widths[:, :, None]).astype(jnp.bfloat16)
        blocked = by_head(vals, heads)
        within = jnp.einsum("hps,hst->hpt", blocked, mixing, preferred_element_type=jnp.float32)
        across = jnp.einsum(
            "cn,nt->ct",
            states.astype(jnp.bfloat16).reshape(vals.shape[0], -1),
            reads,
            preferred_element_type=jnp.float32,
        )
        parts.append(
            within
            + jnp.exp(cum)[:, None, :] * by_head(across, heads)
            + skip_gain[:, None, None] * blocked
        )
        before = before + cum[:, -1]
    return jnp.concatenate(parts, axis=2).reshape(values.shape)


def normalised(mixed, gate_rows, norm_gain):
    gated = mixed * jax.nn.silu(gate_rows)
    scale = lax.rsqrt(jnp.mean(gated * gated, axis=0, keepdims=True) + EPS)
    return (gated * scale * norm_gain[:, None]).astype(jnp.bfloat16)


def earlier_state(hot, fading, tapped, conv_bias, inner):
    heads = fading.shape[0]
    used = (inner + tapped.shape[1]) // 2
    tapped = tapped[:, :used]
    shift = conv_bias[:used, None]

    def of_group(hot, fading):
        rows = jnp.einsum("kc,kt->ct", tapped, hot, precision=THREE) + shift
        active = jax.nn.silu(rows)
        vals = active[:inner].astype(jnp.bfloat16)
        writes = active[inner:].astype(jnp.bfloat16)
        weighted = (by_head(vals, heads) * fading[:, None, :]).astype(jnp.bfloat16)
        return jnp.einsum(
            "cs,ns->cn", weighted.reshape(vals.shape), writes, preferred_element_type=jnp.float32
        )

    tokens = hot.shape[1]
    group = 2048
    if tokens <= group or tokens % group:
        return by_head(of_group(hot, fading), heads)

    def grouped(value):
        return jnp.moveaxis(value.reshape(value.shape[0], -1, group), 1, 0)

    def add(state, item):
        return (state + of_group(*item), None)

    start = jnp.zeros((inner, used - inner), jnp.float32)
    return by_head(lax.scan(add, start, (grouped(hot), grouped(fading)))[0], heads)


def carry_weights(logs):
    parts = logs.shape[0]
    lower = jnp.tril(jnp.ones((parts, parts), jnp.float32))
    inclusive = jnp.einsum("ij,jr->ir", lower, logs, precision=HIGH)
    exclusive = inclusive - logs
    rows = lax.broadcasted_iota(jnp.int32, (parts, parts), 0)
    cols = lax.broadcasted_iota(jnp.int32, (parts, parts), 1)
    keep = (cols > rows)[:, :, None]
    power = exclusive[None, :, :] - inclusive[:, None, :]
    return jnp.where(keep, jnp.exp(jnp.where(keep, power, 0.0)), 0.0)


def settle(state, row_logs, first, second):
    width = state.shape[2]
    parts, span = row_logs.shape
    pieces = lax.all_to_all(
        state.reshape(parts, span, width), "seq", split_axis=0, concat_axis=0, tiled=True
    )
    pieces, first = lax.optimization_barrier((pieces, first))
    settled = jnp.sum(carry_weights(row_logs)[:, :, :, None] * pieces[None], axis=1)
    settled, second = lax.optimization_barrier((settled, second))
    later = lax.all_to_all(settled, "seq", split_axis=0, concat_axis=0, tiled=True)
    return (later.reshape(state.shape), first, second)


def local(
    token_ids,
    input_table,
    gate_table,
    step_table,
    decay_log,
    conv_weight,
    conv_bias,
    skip_gain,
    norm_gain,
    cotangent,
):
    labels = token_ids[0]
    tokens = labels.shape[0]
    width = conv_weight.shape[0]
    vocab, channels = input_table.shape
    inner = gate_table.shape[1]
    heads = step_table.shape[1]
    head = inner // heads
    parts = lax.axis_size("seq")
    index = lax.axis_index("seq")
    own_hot = indicator(labels, vocab)
    step_rows = jnp.einsum("vh,vt->ht", step_table, own_hot, precision=HIGH)
    (steps, log_decay), pull_decays = jax.vjp(decays, step_rows, decay_log)
    rim = width - 1
    heard = lax.all_to_all(
        jnp.broadcast_to(labels[None], (parts, tokens)),
        "seq",
        split_axis=0,
        concat_axis=0,
        tiled=True,
    )
    numbers = jnp.arange(parts, dtype=jnp.int32)
    previous = (numbers == index - 1)[:, None]
    edge = jnp.sum(jnp.where(previous, heard[:, tokens - rim :] + 1, 0), axis=0) - 1
    whole = heard.reshape(parts * tokens)
    padded = jnp.concatenate([jnp.full((rim,), -1, jnp.int32), whole])
    whole_hot = jnp.concatenate(
        [indicator(padded[k : k + parts * tokens], vocab) for k in range(width)]
    )
    whole_steps, whole_logs = decays(
        jnp.einsum("vh,vt->ht", step_table, whole_hot[rim * vocab :], precision=HIGH), decay_log
    )
    lower = jnp.tril(jnp.ones((tokens, tokens), jnp.float32))
    cum = jnp.einsum(
        "hjs,ts->hjt", whole_logs.reshape(heads, parts, tokens), lower, precision=HIGH
    )
    totals = cum[:, :, -1]
    between = (numbers[None, :] > numbers[:, None]) & (numbers[None, :] < index)
    tail = jnp.einsum("jm,hm->hj", between.astype(jnp.float32), totals, precision=HIGH)
    fading = jnp.exp((totals + tail)[:, :, None] - cum) * (numbers < index)[None, :, None]
    fading = fading.reshape(heads, parts * tokens) * whole_steps
    span = inner // parts
    owner = (index * span + jnp.arange(span, dtype=jnp.int32)) // head
    row_logs = jnp.einsum("hj,hr->jr", totals, indicator(owner, heads), precision=HIGH)

    extended = jnp.concatenate([edge, labels])
    hot = jnp.concatenate([indicator(extended[k : k + tokens], vocab) for k in range(width)])
    table = input_table.astype(jnp.float32)
    tapped = (conv_weight[:, None, :] * table[None]).reshape(width * vocab, channels)
    convolved = jnp.einsum("kc,kt->ct", tapped, hot, precision=THREE) + conv_bias[:, None]
    gate_rows = jnp.einsum(
        "vc,vt->ct", gate_table, own_hot.astype(jnp.bfloat16), preferred_element_type=jnp.float32
    )
    (values, write_keys, read_keys), pull_activate = jax.vjp(
        lambda rows: activate(rows, inner), convolved
    )
    (entering, _, total), pull_local = jax.vjp(
        local_states, values, write_keys, steps, log_decay
    )
    carried = earlier_state(whole_hot, fading, tapped, conv_bias, inner)
    mixed, pull_mixed = jax.vjp(
        mixed_rows,
        values,
        write_keys,
        read_keys,
        steps,
        log_decay,
        entering,
        carried,
        skip_gain,
    )
    layer_out, pull_out = jax.vjp(normalised, mixed, gate_rows, norm_gain)
    d_mixed, d_gate, d_norm = pull_out(cotangent[0].T)
    d_values, d_write, d_read, d_steps, d_log, d_entering, d_carried, d_skip = pull_mixed(d_mixed)
    later, (d_values, d_read), d_gate = settle(d_carried, row_logs, (d_values, d_read), d_gate)
    d_total = jnp.exp(total) * jnp.sum(later * carried, axis=(1, 2))
    d_values_state, d_write_state, d_steps_state, d_log_state = pull_local(
        (d_entering, later, d_total)
    )
    (d_convolved,) = pull_activate(
        (d_values + d_values_state, d_write + d_write_state, d_read)
    )
    d_step_rows, d_decay = pull_decays((d_steps + d_steps_state, d_log + d_log_state))
    spread = jnp.einsum("kt,ct->kc", hot, d_convolved, precision=THREE)
    spread = spread.reshape(width, vocab, channels)
    sums = total_over_devices(
        (
            jnp.sum(conv_weight[:, None, :] * spread, axis=0),
            jnp.einsum("vt,ct->vc", own_hot, d_gate, precision=THREE),
            jnp.einsum("vt,ht->vh", own_hot, d_step_rows, precision=HIGH),
            d_decay,
            jnp.sum(table[None] * spread, axis=1),
            jnp.sum(spread[width - 1], axis=0),
            d_skip,
            d_norm,
        )
    )
    return (layer_out.T[None], *sums)


def solution(mesh):
    return jax.shard_map(
        local,
        mesh=mesh,
        in_specs=(
            P("batch", "seq"),
            P(),
            P(),
            P(),
            P(),
            P(),
            P(),
            P(),
            P(),
            P("batch", "seq", None),
        ),
        out_specs=(P("batch", "seq", None), P(), P(), P(), P(), P(), P(), P(), P()),
        check_vma=False,
    )
```
